32 devices in a mesh: outer: 8 (over y, x, core), inner: 4 (over z).
Axes of the slice: x: 2, y: 2, z: 4, core: 2. Of those that a mesh axis runs over, the one named last changes fastest.
Arguments:
- group_latents: bfloat16 [4096, 1024], P(('outer', 'inner')), may hold values from -6 to 6
- slot_ids: int32 [8, 4], P('outer', 'inner'), may hold values from 0 to 3, each once within a row
- slot_embed: bfloat16 [4, 1024], replicated, may hold values from -6 to 6
- merge_latents: bfloat16 [128, 2048], replicated, may hold values from -6 to 6
- query_weight: bfloat16 [2048, 2048], P(None, 'inner'), may hold values from -0.125 to 0.125
- key_weight: bfloat16 [1024, 2048], P(None, 'inner'), may hold values from -0.1875 to 0.1875
- value_weight: bfloat16 [1024, 2048], P(None, 'inner'), may hold values from -0.1875 to 0.1875
- output_weight: bfloat16 [2048, 2048], P('inner'), may hold values from -0.125 to 0.125
- global_latents: bfloat16 [1024, 2048], P(('outer', 'inner')), may hold values from -6 to 6
- decode_query: bfloat16 [2048, 2048], P(None, 'inner'), may hold values from -0.125 to 0.125
- decode_key: bfloat16 [2048, 2048], P(None, 'inner'), may hold values from -0.125 to 0.125
- decode_value: bfloat16 [2048, 2048], P(None, 'inner'), may hold values from -0.125 to 0.125
- decode_output: bfloat16 [2048, 2048], P('inner'), may hold values from -0.125 to 0.125
Outputs:
- decoded: bfloat16 [1024, 2048], P(('outer', 'inner'))
The draws below stay inside these ranges and needn't reach their ends.
Inputs may be any that keep to these rules, and one draw needn't show every extreme that they name: `slot_ids`: each row holds every slot once.
All inputs are finite; a program needn't handle non-finite values.
Results may differ from the reference program's by a relative error of at most 0.014.
Values may be sent and summed in bfloat16 or wider, within the bound.
A program may use at most 64 MiB of HBM per device.

```python
import jax
import jax.numpy as jnp
from jax import lax

D1 = 1024
D2 = 2048
HEAD = 128
L1 = 128
L2 = 128
G3 = 1024
GROUPS = 32
MERGES = 8
N_OUTER = 8
N_INNER = 4


def block_levels(stream_key, dims, cuts, low, top_value):
    loudness = 1.0
    for position, parts in cuts:
        heights = jax.random.uniform(jax.random.fold_in(jax.random.fold_in(stream_key, 6), position), (parts,), jnp.float32, low / len(cuts), top_value / len(cuts))
        loudness = loudness * jnp.repeat(jnp.exp(heights), dims[position] // parts).reshape((-1,) + (1,) * (len(dims) - 1 - position))
    return loudness


def gaussian(rng, shape, deviation, most, split=(), kind=jnp.bfloat16):
    factor_of = block_levels(rng, shape, split, -0.22, 0.18) if split else 1.0
    drawn = jax.random.normal(rng, shape, jnp.float32) * deviation * factor_of
    return jnp.minimum(jnp.maximum(drawn, -most), most).astype(kind)


def setup_inputs(seed: int = 0) -> dict:
    key_list = jax.random.split(jax.random.key(seed), 14)
    group_latents = gaussian(key_list[0], (GROUPS * L1, D1), 1.0, 6.0, ((0, 32),))
    slot_ids = jax.vmap(lambda own: jax.random.permutation(own, N_INNER))(jax.random.split(key_list[1], MERGES)).reshape((MERGES, N_INNER)).astype(jnp.int32)
    slot_embed = gaussian(key_list[2], (N_INNER, D1), 1.0, 6.0)
    merge_latents = gaussian(key_list[3], (L2, D2), 1.0, 6.0)
    query_weight = gaussian(key_list[4], (D2, D2), D2 ** -0.5, 0.125, ((1, 4),))
    key_weight = gaussian(key_list[5], (D1, D2), D1 ** -0.5, 0.1875, ((1, 4),))
    value_weight = gaussian(key_list[6], (D1, D2), D1 ** -0.5, 0.1875, ((1, 4),))
    output_weight = gaussian(key_list[7], (D2, D2), D2 ** -0.5, 0.125, ((0, 4),))
    global_latents = gaussian(key_list[8], (G3, D2), 1.0, 6.0, ((0, 32),))
    decode_query = gaussian(key_list[9], (D2, D2), D2 ** -0.5, 0.125, ((1, 4),))
    decode_key = gaussian(key_list[10], (D2, D2), D2 ** -0.5, 0.125, ((1, 4),))
    decode_value = gaussian(key_list[11], (D2, D2), D2 ** -0.5, 0.125, ((1, 4),))
    decode_output = gaussian(key_list[12], (D2, D2), D2 ** -0.5, 0.125, ((0, 4),))
    return {"group_latents": group_latents, "slot_ids": slot_ids, "slot_embed": slot_embed, "merge_latents": merge_latents, "query_weight": query_weight, "key_weight": key_weight, "value_weight": value_weight, "output_weight": output_weight, "global_latents": global_latents, "decode_query": decode_query, "decode_key": decode_key, "decode_value": decode_value, "decode_output": decode_output}


def attend(query_rows, key_rows, value_rows):
    length = query_rows.shape[0]
    head_count = query_rows.shape[1] // HEAD
    queries = query_rows.reshape(length, head_count, HEAD).astype(jnp.float32)
    keys_in = key_rows.reshape(key_rows.shape[0], head_count, HEAD).astype(jnp.float32)
    values_in = value_rows.reshape(value_rows.shape[0], head_count, HEAD).astype(jnp.float32)
    scores = jnp.einsum('qhd,khd->hqk', queries, keys_in) * HEAD ** (-0.5)
    weights = jax.nn.softmax(scores, axis=-1).astype(jnp.bfloat16)
    mixed = jnp.einsum('hqk,khd->qhd', weights.astype(jnp.float32), values_in)
    return mixed.reshape(length, head_count * HEAD).astype(jnp.bfloat16)

def reference(group_latents, slot_ids, slot_embed, merge_latents, query_weight, key_weight, value_weight, output_weight, global_latents, decode_query, decode_key, decode_value, decode_output):
    slot_rows = jnp.repeat(slot_embed[slot_ids.reshape(-1)], L1, axis=0)
    keyed = (group_latents.astype(jnp.float32) + slot_rows.astype(jnp.float32)).astype(jnp.bfloat16)
    query_two = jnp.dot(merge_latents, query_weight, preferred_element_type=jnp.float32).astype(jnp.bfloat16)
    key_five = jnp.dot(global_latents, decode_key, preferred_element_type=jnp.float32).astype(jnp.bfloat16)
    value_five = jnp.dot(global_latents, decode_value, preferred_element_type=jnp.float32).astype(jnp.bfloat16)

    def one_merge(merged):
        key_two = jnp.dot(merged, key_weight, preferred_element_type=jnp.float32).astype(jnp.bfloat16)
        value_two = jnp.dot(merged, value_weight, preferred_element_type=jnp.float32).astype(jnp.bfloat16)
        mixed_two = attend(query_two, key_two, value_two)
        level_two = merge_latents.astype(jnp.float32) + jnp.dot(mixed_two, output_weight, preferred_element_type=jnp.float32)
        normed = (level_two * lax.rsqrt(lax.optimization_barrier(jnp.mean(level_two * level_two, axis=-1, keepdims=True)) + 1e-06)).astype(jnp.bfloat16)
        query_five = jnp.dot(normed, decode_query, preferred_element_type=jnp.float32).astype(jnp.bfloat16)
        mixed_five = attend(query_five, key_five, value_five)
        return (level_two + jnp.dot(mixed_five, decode_output, preferred_element_type=jnp.float32)).astype(jnp.bfloat16)
    blocks = keyed.reshape(N_OUTER, N_INNER * L1, D1)
    return lax.map(one_merge, blocks).reshape(N_OUTER * L2, D2)
```

```python
import functools

import jax
import jax.numpy as jnp
from jax import lax
from jax.experimental import pallas as pl
from jax.experimental.pallas import tpu as pltpu
from jax.sharding import PartitionSpec as P

HEAD = 128
MESH = pl.DeviceIdType.MESH
F32 = jnp.float32
BF16 = jnp.bfloat16


def multiply(load, weight, store):
    columns = weight.shape[1]
    tile = min(256, columns)

    @pl.loop(0, columns // tile)
    def _(t):
        cols = pl.ds(pl.multiple_of(t * tile, tile), tile)
        store(cols, jnp.dot(load(), weight[:, cols], preferred_element_type=F32))


def flat(blocks):
    count, rows, columns = blocks.shape
    if rows % 16:
        return blocks.astype(F32).reshape(count * rows, columns).astype(BF16)
    return blocks.reshape(count * rows, columns)


def attend_head(query, keys, values):
    scores = lax.dot_general(
        query, keys, (((1,), (1,)), ((), ())), preferred_element_type=F32
    ) * (HEAD ** -0.5)
    top = jnp.max(scores, axis=-1, keepdims=True)
    raised = jnp.exp(scores - top)
    total = jnp.sum(raised, axis=-1, keepdims=True)
    mixed = jnp.dot(raised.astype(BF16), values, preferred_element_type=F32)
    return (mixed / total).astype(BF16)


class Chain:
    def __init__(self, buf, up, down, recv, me, count):
        self.buf, self.up, self.down, self.recv = buf, up, down, recv
        self.me, self.count = me, count

    def copy(self, block, sems, target):
        return pltpu.make_async_remote_copy(
            src_ref=self.buf.at[block],
            dst_ref=self.buf.at[block],
            send_sem=sems.at[block],
            recv_sem=self.recv.at[block],
            device_id={"inner": target},
            device_id_type=MESH,
        )

    def send_up(self, block):
        @pl.when(self.me < self.count - 1)
        def _():
            self.copy(block, self.up, self.me + 1).start()

    def send_down(self, block):
        @pl.when(self.me > 0)
        def _():
            self.copy(block, self.down, self.me - 1).start()

    def begin(self):
        self.send_up(self.me)
        self.send_down(self.me)

    def step(self, s, work=None):
        low, high = self.me - s, self.me + s

        @pl.when(low >= 0)
        def _():
            self.copy(low, self.up, self.me - 1).wait_recv()
            self.send_up(low)

        @pl.when(high < self.count)
        def _():
            self.copy(high, self.down, self.me + 1).wait_recv()
            self.send_down(high)

        if work is not None:

            @pl.when(low >= 0)
            def _():
                work(low)

            @pl.when(high < self.count)
            def _():
                work(high)

    def drain(self):
        for b in range(self.count):

            @pl.when((self.me >= b) & (self.me < self.count - 1))
            def _():
                self.copy(b, self.up, self.me + 1).wait_send()

            @pl.when((self.me <= b) & (self.me > 0))
            def _():
                self.copy(b, self.down, self.me - 1).wait_send()


class Scatter:
    def __init__(self, source, landing, send, recv, me, count):
        self.source, self.landing, self.send, self.recv = source, landing, send, recv
        self.me, self.count = me, count

    def copy(self, hop):
        target = lax.rem(self.me + hop, self.count)
        return pltpu.make_async_remote_copy(
            src_ref=self.source.at[target],
            dst_ref=self.landing.at[hop],
            send_sem=self.send.at[hop],
            recv_sem=self.recv.at[hop],
            device_id={"inner": target},
            device_id_type=MESH,
        )

    def begin(self):
        for hop in range(1, self.count):
            self.copy(hop).start()

    def total(self, own):
        total = own + self.source[self.me].astype(F32)
        for hop in range(1, self.count):
            self.copy(hop).wait_recv()
            total = total + self.landing[hop].astype(F32)
        return total

    def drain(self):
        for hop in range(1, self.count):
            self.copy(hop).wait_send()


def kernel(
    inner, outer,
    slot_in, group_in, embed_in, merge_in, qw_in, kw_in, vw_in, ow_in,
    global_in, dq_in, dk_in, dv_in, do_in,
    out_ref,
    embed, merge, group, qw, kw, vw, ow, dq, dk, dv, do,
    keyed, glob, key_two, value_two, query, mixed, merge_rows, level, pairs, normed,
    term_a, land_a, term_b, land_b,
    load_sem, k_up, k_down, k_recv, g_up, g_down, g_recv, n_up, n_down, n_recv,
    a_send, a_recv, b_send, b_recv, p_send, p_pass, p_recv,
):
    me = lax.axis_index("inner")
    place = lax.axis_index("outer")
    chips = outer // 2
    chip, core = place // 2, lax.rem(place, 2)
    width = qw.shape[1]
    heads = width // HEAD

    loads = [
        pltpu.make_async_copy(src, dst, load_sem.at[n])
        for n, (src, dst) in enumerate([
            (group_in, group), (embed_in, embed), (global_in, glob.at[me]), (merge_in, merge),
            (qw_in, qw), (kw_in, kw), (vw_in, vw), (ow_in, ow),
            (dk_in, dk), (dv_in, dv), (dq_in, dq), (do_in, do),
        ])
    ]
    for load in loads:
        load.start()

    barrier = pltpu.get_barrier_semaphore()
    for hop in range(1, inner):
        pl.semaphore_signal(
            barrier, inc=1, device_id={"inner": lax.rem(me + hop, inner)}, device_id_type=MESH
        )
    for hop in range(1, chips):
        pl.semaphore_signal(
            barrier, inc=1,
            device_id={"outer": lax.rem(chip + hop, chips) * 2 + core}, device_id_type=MESH,
        )
    partner = chip * 2 + 1 - core
    pl.semaphore_signal(barrier, inc=1, device_id={"outer": partner}, device_id_type=MESH)

    for n in (0, 1):
        loads[n].wait()
    slot = slot_in[0, 0]
    rows = lax.broadcasted_iota(jnp.int32, embed.shape, 0)
    vector = jnp.sum(
        jnp.where(rows == slot, embed[...].astype(F32), 0.0), axis=0, keepdims=True
    )
    keyed[me] = (group[...].astype(F32) + vector).astype(BF16)
    pl.semaphore_wait(barrier, inner - 1 + chips)

    chain_k = Chain(keyed, k_up, k_down, k_recv, me, inner)
    chain_g = Chain(glob, g_up, g_down, g_recv, me, inner)
    chain_n = Chain(normed, n_up, n_down, n_recv, me, inner)
    sum_a = Scatter(term_a, land_a, a_send, a_recv, me, inner)
    sum_b = Scatter(term_b, land_b, b_send, b_recv, me, inner)

    chain_k.begin()

    for n in (2, 3, 4):
        loads[n].wait()
    merge_rows[...] = merge[...].astype(F32).reshape(merge_rows.shape)

    def put_query(cols, value):
        query[:, cols] = value.astype(BF16)

    multiply(lambda: merge[...], qw, put_query)

    for n in (5, 6):
        loads[n].wait()

    def keys_values(block):
        def put_key(cols, value):
            key_two[block, :, cols] = value.astype(BF16)

        def put_value(cols, value):
            value_two[block, :, cols] = value.astype(BF16)

        multiply(lambda: keyed[block], kw, put_key)
        multiply(lambda: keyed[block], vw, put_value)

    keys_values(me)
    for s in range(1, inner):
        if s == inner - 1:
            chain_k.step(s)
            chain_g.begin()

            @pl.when(me - s >= 0)
            def _():
                keys_values(me - s)

            @pl.when(me + s < inner)
            def _():
                keys_values(me + s)
        else:
            chain_k.step(s, keys_values)

    steps = list(range(1, inner))
    for h in range(heads):
        cols = slice(h * HEAD, (h + 1) * HEAD)
        mixed[:, cols] = attend_head(
            query[:, cols], flat(key_two[:, :, cols]), flat(value_two[:, :, cols])
        )
        if h % 2 and steps:
            chain_g.step(steps.pop(0))

    loads[7].wait()

    def put_term(term):
        def put(cols, value):
            term[:, :, cols] = value.reshape(
                inner, term.shape[1], value.shape[1]
            ).astype(BF16)

        return put

    multiply(lambda: mixed[...], ow, put_term(term_a))
    sum_a.begin()

    for s in steps:
        chain_g.step(s)
    for n in (8, 9):
        loads[n].wait()

    def put_pair(start):
        def put(cols, value):
            shifted = pl.ds(pl.multiple_of(cols.start + start, HEAD), cols.size)
            pairs[place, :, shifted] = value.astype(BF16)

        return put

    multiply(lambda: flat(glob[...]), dk, put_pair(0))
    multiply(lambda: flat(glob[...]), dv, put_pair(width))

    def direct(hop):
        target = lax.rem(chip + hop, chips) * 2 + core
        return pltpu.make_async_remote_copy(
            src_ref=pairs.at[place], dst_ref=pairs.at[place],
            send_sem=p_send.at[hop], recv_sem=p_recv.at[place],
            device_id={"outer": target}, device_id_type=MESH,
        )

    def arrival(block):
        return pltpu.make_async_remote_copy(
            src_ref=pairs.at[block], dst_ref=pairs.at[block],
            send_sem=p_pass.at[0], recv_sem=p_recv.at[block],
            device_id={"outer": partner}, device_id_type=MESH,
        )

    def onward(hop):
        block = lax.rem(chip + hop, chips) * 2 + core
        return pltpu.make_async_remote_copy(
            src_ref=pairs.at[block], dst_ref=pairs.at[block],
            send_sem=p_pass.at[hop], recv_sem=p_recv.at[block],
            device_id={"outer": partner}, device_id_type=MESH,
        )

    for hop in range(1, chips):
        direct(hop).start()
    onward(0).start()

    own = sum_a.total(merge_rows[me])
    level[...] = own
    scale = lax.rsqrt(jnp.mean(own * own, axis=-1, keepdims=True) + 1e-6)
    normed[me] = (own * scale).astype(BF16)
    chain_n.begin()
    for s in range(1, inner):
        chain_n.step(s)
    loads[10].wait()
    multiply(lambda: flat(normed[...]), dq, put_query)

    for hop in range(1, chips):
        arrival(lax.rem(chip + hop, chips) * 2 + core).wait_recv()
        onward(hop).start()
    for hop in range(chips):
        arrival(lax.rem(chip + hop, chips) * 2 + 1 - core).wait_recv()

    for h in range(heads):
        cols = slice(h * HEAD, (h + 1) * HEAD)
        after = slice(width + h * HEAD, width + (h + 1) * HEAD)
        mixed[:, cols] = attend_head(
            query[:, cols], flat(pairs[:, :, cols]), flat(pairs[:, :, after])
        )
    loads[11].wait()
    multiply(lambda: mixed[...], do, put_term(term_b))
    sum_b.begin()

    chain_k.drain()
    chain_g.drain()
    chain_n.drain()
    sum_a.drain()
    for hop in range(1, chips):
        direct(hop).wait_send()
    for hop in range(chips):
        onward(hop).wait_send()
    out_ref[...] = sum_b.total(level[...]).astype(BF16)
    sum_b.drain()


def local(inner, outer, group, slot_ids, embed, merge, qw, kw, vw, ow, glob, dq, dk, dv, do):
    rows, depth = group.shape
    queries, wide = merge.shape
    width = qw.shape[1]
    own = queries // inner
    blocks = glob.shape[0] * inner
    dma = pltpu.SemaphoreType.DMA
    vmem = lambda *shape, kind=BF16: pltpu.VMEM(shape, kind)
    same = lambda array: pltpu.VMEM(array.shape, array.dtype)
    scratch = [
        same(embed), same(merge), same(group), same(qw), same(kw), same(vw), same(ow),
        same(dq), same(dk), same(dv), same(do),
        vmem(inner, rows, depth),
        vmem(inner, glob.shape[0], wide),
        vmem(inner, rows, width),
        vmem(inner, rows, width),
        vmem(queries, width),
        vmem(queries, width),
        vmem(inner, own, wide, kind=F32),
        vmem(own, wide, kind=F32),
        vmem(outer, blocks, 2 * width),
        vmem(inner, own, wide),
        vmem(inner, own, wide), vmem(inner, own, wide),
        vmem(inner, own, wide), vmem(inner, own, wide),
        dma((12,)),
    ] + [dma((inner,))] * 13 + [dma((outer // 2,))] * 2 + [dma((outer,))]
    any_space = pl.BlockSpec(memory_space=pl.ANY)
    return pl.pallas_call(
        functools.partial(kernel, inner, outer),
        out_shape=jax.ShapeDtypeStruct((own, wide), BF16),
        in_specs=[pl.BlockSpec(memory_space=pltpu.SMEM)] + [any_space] * 12,
        out_specs=pl.BlockSpec(memory_space=pltpu.VMEM),
        scratch_shapes=scratch,
        compiler_params=pltpu.CompilerParams(
            collective_id=0, has_side_effects=True, vmem_limit_bytes=56 * 2 ** 20
        ),
    )(slot_ids, group, embed, merge, qw, kw, vw, ow, glob, dq, dk, dv, do)


def solution(mesh):
    rows = P(("outer", "inner"), None)
    split = P(None, "inner")
    down = P("inner", None)
    return jax.shard_map(
        functools.partial(local, mesh.shape["inner"], mesh.shape["outer"]),
        mesh=mesh,
        in_specs=(
            rows, P("outer", "inner"), P(), P(), split, split, split, down,
            rows, split, split, split, down,
        ),
        out_specs=rows,
        check_vma=False,
    )
```

```python
import functools

import jax
import jax.numpy as jnp
from jax import lax
from jax.experimental import pallas as pl
from jax.experimental.pallas import tpu as pltpu
from jax.sharding import PartitionSpec as P

HEAD = 128
MESH = pl.DeviceIdType.MESH
F32 = jnp.float32
BF16 = jnp.bfloat16


def multiply(load, weight, store):
    columns = weight.shape[1]
    tile = min(256, columns)

    @pl.loop(0, columns // tile)
    def _(t):
        cols = pl.ds(pl.multiple_of(t * tile, tile), tile)
        store(cols, jnp.dot(load(), weight[:, cols], preferred_element_type=F32))


def flat(blocks):
    count, rows, columns = blocks.shape
    if rows % 16:
        return blocks.astype(F32).reshape(count * rows, columns).astype(BF16)
    return blocks.reshape(count * rows, columns)


def attend_head(query, keys, values):
    scores = lax.dot_general(
        query, keys, (((1,), (1,)), ((), ())), preferred_element_type=F32
    ) * (HEAD ** -0.5)
    top = jnp.max(scores, axis=-1, keepdims=True)
    raised = jnp.exp(scores - top)
    total = jnp.sum(raised, axis=-1, keepdims=True)
    mixed = jnp.dot(raised.astype(BF16), values, preferred_element_type=F32)
    return (mixed / total).astype(BF16)


class Spread:
    def __init__(self, buf, up, down, recv, me, count):
        self.buf, self.up, self.down, self.recv = buf, up, down, recv
        self.me, self.count = me, count

    def copy(self, block, sem, target):
        return pltpu.make_async_remote_copy(
            src_ref=self.buf.at[block],
            dst_ref=self.buf.at[block],
            send_sem=sem,
            recv_sem=self.recv.at[block],
            device_id={"inner": target},
            device_id_type=MESH,
        )

    def own(self, act):
        for hop in range(self.count - 1, 0, -1):
            last = 1 if hop == 1 else 2

            @pl.when(self.me + hop <= self.count - last)
            def _():
                act(self.copy(self.me, self.up.at[hop, 0], self.me + hop))

            @pl.when(self.me - hop >= last - 1)
            def _():
                act(self.copy(self.me, self.down.at[hop, 0], self.me - hop))

    def begin(self):
        self.own(lambda copy: copy.start())

    def onward(self, s, act):
        @pl.when((self.me == self.count - 2) & (self.me - s >= 0))
        def _():
            act(self.copy(self.me - s, self.up.at[s, 1], self.count - 1))

        @pl.when((self.me == 1) & (self.me + s < self.count))
        def _():
            act(self.copy(self.me + s, self.down.at[s, 1], 0))

    def step(self, s, work=None):
        low, high = self.me - s, self.me + s

        @pl.when(low >= 0)
        def _():
            self.copy(low, self.up.at[s, 1], self.me - 1).wait_recv()

        @pl.when(high < self.count)
        def _():
            self.copy(high, self.down.at[s, 1], self.me + 1).wait_recv()

        self.onward(s, lambda copy: copy.start())
        if work is not None:

            @pl.when(low >= 0)
            def _():
                work(low)

            @pl.when(high < self.count)
            def _():
                work(high)

    def drain(self):
        self.own(lambda copy: copy.wait_send())
        for s in range(1, self.count):
            self.onward(s, lambda copy: copy.wait_send())


class Scatter:
    def __init__(self, term, relay, landing, send, recv, passed, me, count):
        self.term, self.relay, self.landing = term, relay, landing
        self.send, self.recv, self.passed = send, recv, passed
        self.me, self.count = me, count

    def to(self, block, target):
        return pltpu.make_async_remote_copy(
            src_ref=self.term.at[block],
            dst_ref=self.landing.at[self.me],
            send_sem=self.send.at[block],
            recv_sem=self.recv.at[self.me],
            device_id={"inner": target},
            device_id_type=MESH,
        )

    def via(self, block, target):
        return pltpu.make_async_remote_copy(
            src_ref=self.term.at[block],
            dst_ref=self.relay.at[block],
            send_sem=self.send.at[block],
            recv_sem=self.passed.at[block],
            device_id={"inner": target},
            device_id_type=MESH,
        )

    def came(self, source):
        pltpu.make_async_remote_copy(
            src_ref=self.landing.at[source],
            dst_ref=self.landing.at[source],
            send_sem=self.send.at[source],
            recv_sem=self.recv.at[source],
            device_id={"inner": source},
            device_id_type=MESH,
        ).wait_recv()

    def add(self, block, end):
        self.via(block, end).wait_recv()
        self.term[block] = (
            self.term[block].astype(F32) + self.relay[block].astype(F32)
        ).astype(BF16)
        self.to(block, block).start()

    def run(self):
        count, me = self.count, self.me

        @pl.when(me == 0)
        def _():
            for block in range(count - 1, 1, -1):
                self.via(block, 1).start()
            self.to(1, 1).start()

        @pl.when(me == count - 1)
        def _():
            for block in range(count - 2):
                self.via(block, count - 2).start()
            self.to(count - 2, count - 2).start()

        for far in range(count):

            @pl.when((me > 0) & (me < count - 2) & (count - 1 - far > me) & (me > 1))
            def _():
                self.to(count - 1 - far, count - 1 - far).start()

            @pl.when((me == count - 2) & (count - 1 - far > me))
            def _():
                self.to(count - 1 - far, count - 1 - far).start()

            @pl.when((me > 1) & (me < count - 2) & (far < me))
            def _():
                self.to(far, far).start()

            @pl.when((me == 1) & (far < me))
            def _():
                self.to(far, far).start()

        @pl.when(me == 1)
        def _():
            for block in range(count - 1, 1, -1):
                self.add(block, 0)

        @pl.when(me == count - 2)
        def _():
            for block in range(count - 2):
                self.add(block, count - 1)

    def total(self, own, into):
        into[...] = own + self.term[self.me].astype(F32)
        for source in range(self.count):
            there = self.me != source
            if source == 0:
                there = self.me == 1
            if source == self.count - 1:
                there = self.me == self.count - 2

            @pl.when(there)
            def _():
                self.came(source)
                into[...] += self.landing[source].astype(F32)

    def drain(self):
        for block in range(self.count):

            @pl.when(self.me != block)
            def _():
                self.to(block, block).wait_send()


def kernel(
    inner, outer,
    slot_in, group_in, embed_in, merge_in, qw_in, kw_in, vw_in, ow_in,
    global_in, dq_in, dk_in, dv_in, do_in,
    out_ref,
    embed, merge, group, qw, kw, vw, ow, dq, dk, dv, do,
    keyed, glob, key_two, value_two, query, mixed, merge_rows, level, pairs, normed,
    term_a, relay_a, land_a, term_b, relay_b, land_b,
    load_sem, k_up, k_down, k_recv, g_up, g_down, g_recv, n_up, n_down, n_recv,
    a_send, a_recv, a_pass, b_send, b_recv, b_pass, p_send, p_pass, p_recv,
):
    me = lax.axis_index("inner")
    place = lax.axis_index("outer")
    chips = outer // 2
    chip, core = place // 2, lax.rem(place, 2)
    width = qw.shape[1]
    heads = width // HEAD

    loads = [
        pltpu.make_async_copy(src, dst, load_sem.at[n])
        for n, (src, dst) in enumerate([
            (group_in, group), (embed_in, embed), (global_in, glob.at[me]), (merge_in, merge),
            (qw_in, qw), (kw_in, kw), (vw_in, vw), (ow_in, ow),
            (dk_in, dk), (dv_in, dv), (dq_in, dq), (do_in, do),
        ])
    ]
    for load in loads:
        load.start()

    barrier = pltpu.get_barrier_semaphore()
    for hop in range(1, inner):
        pl.semaphore_signal(
            barrier, inc=1, device_id={"inner": lax.rem(me + hop, inner)}, device_id_type=MESH
        )
    for hop in range(1, chips):
        pl.semaphore_signal(
            barrier, inc=1,
            device_id={"outer": lax.rem(chip + hop, chips) * 2 + core}, device_id_type=MESH,
        )
    partner = chip * 2 + 1 - core
    pl.semaphore_signal(barrier, inc=1, device_id={"outer": partner}, device_id_type=MESH)

    for n in (0, 1):
        loads[n].wait()
    slot = slot_in[0, 0]
    rows = lax.broadcasted_iota(jnp.int32, embed.shape, 0)
    vector = jnp.sum(
        jnp.where(rows == slot, embed[...].astype(F32), 0.0), axis=0, keepdims=True
    )
    keyed[me] = (group[...].astype(F32) + vector).astype(BF16)
    pl.semaphore_wait(barrier, inner - 1 + chips)

    chain_k = Spread(keyed, k_up, k_down, k_recv, me, inner)
    chain_g = Spread(glob, g_up, g_down, g_recv, me, inner)
    chain_n = Spread(normed, n_up, n_down, n_recv, me, inner)
    sum_a = Scatter(term_a, relay_a, land_a, a_send, a_recv, a_pass, me, inner)
    sum_b = Scatter(term_b, relay_b, land_b, b_send, b_recv, b_pass, me, inner)

    chain_k.begin()

    for n in (2, 3, 4):
        loads[n].wait()
    merge_rows[...] = merge[...].astype(F32).reshape(merge_rows.shape)

    def put_query(cols, value):
        query[:, cols] = value.astype(BF16)

    multiply(lambda: merge[...], qw, put_query)

    for n in (5, 6):
        loads[n].wait()

    def keys_values(block):
        def put_key(cols, value):
            key_two[block, :, cols] = value.astype(BF16)

        def put_value(cols, value):
            value_two[block, :, cols] = value.astype(BF16)

        multiply(lambda: keyed[block], kw, put_key)
        multiply(lambda: keyed[block], vw, put_value)

    chain_g.begin()
    keys_values(me)
    for s in range(1, inner):
        if s == inner - 1:
            chain_k.step(s)

            @pl.when(me - s >= 0)
            def _():
                keys_values(me - s)

            @pl.when(me + s < inner)
            def _():
                keys_values(me + s)
        else:
            chain_k.step(s, keys_values)

    steps = list(range(1, inner))
    for h in range(heads):
        cols = slice(h * HEAD, (h + 1) * HEAD)
        mixed[:, cols] = attend_head(
            query[:, cols], flat(key_two[:, :, cols]), flat(value_two[:, :, cols])
        )
        if h % 2 and steps:
            chain_g.step(steps.pop(0))

    loads[7].wait()

    def put_term(term):
        def put(cols, value):
            term[:, :, cols] = value.reshape(
                inner, term.shape[1], value.shape[1]
            ).astype(BF16)

        return put

    multiply(lambda: mixed[...], ow, put_term(term_a))
    sum_a.run()

    for s in steps:
        chain_g.step(s)
    for n in (8, 9):
        loads[n].wait()

    def put_pair(start):
        def put(cols, value):
            shifted = pl.ds(pl.multiple_of(cols.start + start, HEAD), cols.size)
            pairs[place, :, shifted] = value.astype(BF16)

        return put

    multiply(lambda: flat(glob[...]), dk, put_pair(0))
    multiply(lambda: flat(glob[...]), dv, put_pair(width))

    def direct(hop):
        target = lax.rem(chip + hop, chips) * 2 + core
        return pltpu.make_async_remote_copy(
            src_ref=pairs.at[place], dst_ref=pairs.at[place],
            send_sem=p_send.at[hop], recv_sem=p_recv.at[place],
            device_id={"outer": target}, device_id_type=MESH,
        )

    def arrival(block):
        return pltpu.make_async_remote_copy(
            src_ref=pairs.at[block], dst_ref=pairs.at[block],
            send_sem=p_pass.at[0], recv_sem=p_recv.at[block],
            device_id={"outer": partner}, device_id_type=MESH,
        )

    def onward(hop):
        block = lax.rem(chip + hop, chips) * 2 + core
        return pltpu.make_async_remote_copy(
            src_ref=pairs.at[block], dst_ref=pairs.at[block],
            send_sem=p_pass.at[hop], recv_sem=p_recv.at[block],
            device_id={"outer": partner}, device_id_type=MESH,
        )

    for hop in range(1, chips):
        direct(hop).start()
    onward(0).start()

    sum_a.total(merge_rows[me], level)
    own = level[...]
    scale = lax.rsqrt(jnp.mean(own * own, axis=-1, keepdims=True) + 1e-6)
    normed[me] = (own * scale).astype(BF16)
    chain_n.begin()
    for hop in range(1, chips):
        arrival(lax.rem(chip + hop, chips) * 2 + core).wait_recv()
        onward(hop).start()
    for s in range(1, inner):
        chain_n.step(s)
    loads[10].wait()
    multiply(lambda: flat(normed[...]), dq, put_query)

    for hop in range(chips):
        arrival(lax.rem(chip + hop, chips) * 2 + 1 - core).wait_recv()

    for h in range(heads):
        cols = slice(h * HEAD, (h + 1) * HEAD)
        after = slice(width + h * HEAD, width + (h + 1) * HEAD)
        mixed[:, cols] = attend_head(
            query[:, cols], flat(pairs[:, :, cols]), flat(pairs[:, :, after])
        )
    loads[11].wait()
    multiply(lambda: mixed[...], do, put_term(term_b))
    sum_b.run()

    chain_k.drain()
    chain_g.drain()
    chain_n.drain()
    sum_a.drain()
    for hop in range(1, chips):
        direct(hop).wait_send()
    for hop in range(chips):
        onward(hop).wait_send()
    sum_b.total(level[...], level)
    out_ref[...] = level[...].astype(BF16)
    sum_b.drain()


def local(inner, outer, group, slot_ids, embed, merge, qw, kw, vw, ow, glob, dq, dk, dv, do):
    rows, depth = group.shape
    queries, wide = merge.shape
    width = qw.shape[1]
    own = queries // inner
    blocks = glob.shape[0] * inner
    dma = pltpu.SemaphoreType.DMA
    vmem = lambda *shape, kind=BF16: pltpu.VMEM(shape, kind)
    same = lambda array: pltpu.VMEM(array.shape, array.dtype)
    scratch = [
        same(embed), same(merge), same(group), same(qw), same(kw), same(vw), same(ow),
        same(dq), same(dk), same(dv), same(do),
        vmem(inner, rows, depth),
        vmem(inner, glob.shape[0], wide),
        vmem(inner, rows, width),
        vmem(inner, rows, width),
        vmem(queries, width),
        vmem(queries, width),
        vmem(inner, own, wide, kind=F32),
        vmem(own, wide, kind=F32),
        vmem(outer, blocks, 2 * width),
        vmem(inner, own, wide),
    ] + [vmem(inner, own, wide)] * 6 + [
        dma((12,)),
    ] + [dma((inner, 2)), dma((inner, 2)), dma((inner,))] * 3 + [dma((inner,))] * 6 + [dma((outer // 2,))] * 2 + [dma((outer,))]
    any_space = pl.BlockSpec(memory_space=pl.ANY)
    return pl.pallas_call(
        functools.partial(kernel, inner, outer),
        out_shape=jax.ShapeDtypeStruct((own, wide), BF16),
        in_specs=[pl.BlockSpec(memory_space=pltpu.SMEM)] + [any_space] * 12,
        out_specs=pl.BlockSpec(memory_space=pltpu.VMEM),
        scratch_shapes=scratch,
        compiler_params=pltpu.CompilerParams(
            collective_id=0, has_side_effects=True, vmem_limit_bytes=56 * 2 ** 20
        ),
    )(slot_ids, group, embed, merge, qw, kw, vw, ow, glob, dq, dk, dv, do)


def solution(mesh):
    rows = P(("outer", "inner"), None)
    split = P(None, "inner")
    down = P("inner", None)
    return jax.shard_map(
        functools.partial(local, mesh.shape["inner"], mesh.shape["outer"]),
        mesh=mesh,
        in_specs=(
            rows, P("outer", "inner"), P(), P(), split, split, split, down,
            rows, split, split, split, down,
        ),
        out_specs=rows,
        check_vma=False,
    )
```

```python
import functools

import jax
import jax.numpy as jnp
from jax import lax
from jax.experimental import pallas as pl
from jax.experimental.pallas import tpu as pltpu
from jax.sharding import PartitionSpec as P

HEAD = 128
MESH = pl.DeviceIdType.MESH
F32 = jnp.float32
BF16 = jnp.bfloat16


def multiply(load, weight, store):
    columns = weight.shape[1]
    tile = min(512, columns)

    @pl.loop(0, columns // tile)
    def _(t):
        cols = pl.ds(pl.multiple_of(t * tile, tile), tile)
        store(cols, jnp.dot(load(), weight[:, cols], preferred_element_type=F32))


def flat(blocks):
    count, rows, columns = blocks.shape
    if rows % 16:
        return blocks.astype(F32).reshape(count * rows, columns).astype(BF16)
    return blocks.reshape(count * rows, columns)


def attend_head(query, keys, values):
    scores = lax.dot_general(
        query, keys, (((1,), (1,)), ((), ())), preferred_element_type=F32
    ) * (HEAD ** -0.5)
    top = jnp.max(scores, axis=-1, keepdims=True)
    raised = jnp.exp(scores - top)
    total = jnp.sum(raised, axis=-1, keepdims=True)
    mixed = jnp.dot(raised.astype(BF16), values, preferred_element_type=F32)
    return (mixed / total).astype(BF16)


class Spread:
    def __init__(self, buf, up, down, recv, me, count):
        self.buf, self.up, self.down, self.recv = buf, up, down, recv
        self.me, self.count = me, count

    def copy(self, block, sem, target):
        return pltpu.make_async_remote_copy(
            src_ref=self.buf.at[block],
            dst_ref=self.buf.at[block],
            send_sem=sem,
            recv_sem=self.recv.at[block],
            device_id={"inner": target},
            device_id_type=MESH,
        )

    def own(self, act):
        for hop in range(self.count - 1, 0, -1):
            last = 1 if hop == 1 else 2

            @pl.when(self.me + hop <= self.count - last)
            def _():
                act(self.copy(self.me, self.up.at[hop, 0], self.me + hop))

            @pl.when(self.me - hop >= last - 1)
            def _():
                act(self.copy(self.me, self.down.at[hop, 0], self.me - hop))

    def begin(self):
        self.own(lambda copy: copy.start())

    def onward(self, s, act):
        @pl.when((self.me == self.count - 2) & (self.me - s >= 0))
        def _():
            act(self.copy(self.me - s, self.up.at[s, 1], self.count - 1))

        @pl.when((self.me == 1) & (self.me + s < self.count))
        def _():
            act(self.copy(self.me + s, self.down.at[s, 1], 0))

    def step(self, s, work=None):
        low, high = self.me - s, self.me + s

        @pl.when(low >= 0)
        def _():
            self.copy(low, self.up.at[s, 1], self.me - 1).wait_recv()

        @pl.when(high < self.count)
        def _():
            self.copy(high, self.down.at[s, 1], self.me + 1).wait_recv()

        self.onward(s, lambda copy: copy.start())
        if work is not None:

            @pl.when(low >= 0)
            def _():
                work(low)

            @pl.when(high < self.count)
            def _():
                work(high)

    def drain(self):
        self.own(lambda copy: copy.wait_send())
        for s in range(1, self.count):
            self.onward(s, lambda copy: copy.wait_send())


class Scatter:
    def __init__(self, term, relay, landing, send, recv, passed, me, count):
        self.term, self.relay, self.landing = term, relay, landing
        self.send, self.recv, self.passed = send, recv, passed
        self.me, self.count = me, count

    def to(self, block, target):
        return pltpu.make_async_remote_copy(
            src_ref=self.term.at[block],
            dst_ref=self.landing.at[self.me],
            send_sem=self.send.at[block],
            recv_sem=self.recv.at[self.me],
            device_id={"inner": target},
            device_id_type=MESH,
        )

    def via(self, block, target):
        return pltpu.make_async_remote_copy(
            src_ref=self.term.at[block],
            dst_ref=self.relay.at[block],
            send_sem=self.send.at[block],
            recv_sem=self.passed.at[block],
            device_id={"inner": target},
            device_id_type=MESH,
        )

    def came(self, source):
        pltpu.make_async_remote_copy(
            src_ref=self.landing.at[source],
            dst_ref=self.landing.at[source],
            send_sem=self.send.at[source],
            recv_sem=self.recv.at[source],
            device_id={"inner": source},
            device_id_type=MESH,
        ).wait_recv()

    def add(self, block, end):
        self.via(block, end).wait_recv()
        self.term[block] = (
            self.term[block].astype(F32) + self.relay[block].astype(F32)
        ).astype(BF16)
        self.to(block, block).start()

    def run(self):
        count, me = self.count, self.me

        @pl.when(me == 0)
        def _():
            for block in range(count - 1, 1, -1):
                self.via(block, 1).start()
            self.to(1, 1).start()

        @pl.when(me == count - 1)
        def _():
            for block in range(count - 2):
                self.via(block, count - 2).start()
            self.to(count - 2, count - 2).start()

        for far in range(count):

            @pl.when((me > 0) & (me < count - 2) & (count - 1 - far > me) & (me > 1))
            def _():
                self.to(count - 1 - far, count - 1 - far).start()

            @pl.when((me == count - 2) & (count - 1 - far > me))
            def _():
                self.to(count - 1 - far, count - 1 - far).start()

            @pl.when((me > 1) & (me < count - 2) & (far < me))
            def _():
                self.to(far, far).start()

            @pl.when((me == 1) & (far < me))
            def _():
                self.to(far, far).start()

        @pl.when(me == 1)
        def _():
            for block in range(count - 1, 1, -1):
                self.add(block, 0)

        @pl.when(me == count - 2)
        def _():
            for block in range(count - 2):
                self.add(block, count - 1)

    def total(self, own, into):
        into[...] = own + self.term[self.me].astype(F32)
        for source in range(self.count):
            there = self.me != source
            if source == 0:
                there = self.me == 1
            if source == self.count - 1:
                there = self.me == self.count - 2

            @pl.when(there)
            def _():
                self.came(source)
                into[...] += self.landing[source].astype(F32)

    def drain(self):
        for block in range(self.count):

            @pl.when(self.me != block)
            def _():
                self.to(block, block).wait_send()


def kernel(
    inner, outer,
    slot_in, group_in, embed_in, merge_in, qw_in, kw_in, vw_in, ow_in,
    global_in, dq_in, dk_in, dv_in, do_in,
    out_ref,
    embed, merge, group, qw, kw, vw, ow, dq, dk, dv, do,
    keyed, glob, key_two, value_two, query, mixed, merge_rows, level, pairs, normed,
    term_a, relay_a, land_a, term_b, relay_b, land_b,
    load_sem, k_up, k_down, k_recv, g_up, g_down, g_recv, n_up, n_down, n_recv,
    a_send, a_recv, a_pass, b_send, b_recv, b_pass, p_send, p_pass, p_recv,
):
    me = lax.axis_index("inner")
    place = lax.axis_index("outer")
    chips = outer // 2
    chip, core = place // 2, lax.rem(place, 2)
    width = qw.shape[1]
    heads = width // HEAD

    loads = [
        pltpu.make_async_copy(src, dst, load_sem.at[n])
        for n, (src, dst) in enumerate([
            (group_in, group), (embed_in, embed), (global_in, glob.at[me]), (merge_in, merge),
            (qw_in, qw), (kw_in, kw), (vw_in, vw), (ow_in, ow),
            (dk_in, dk), (dv_in, dv), (dq_in, dq), (do_in, do),
        ])
    ]
    for load in loads:
        load.start()

    barrier = pltpu.get_barrier_semaphore()
    for hop in range(1, inner):
        pl.semaphore_signal(
            barrier, inc=1, device_id={"inner": lax.rem(me + hop, inner)}, device_id_type=MESH
        )
    for hop in range(1, chips):
        pl.semaphore_signal(
            barrier, inc=1,
            device_id={"outer": lax.rem(chip + hop, chips) * 2 + core}, device_id_type=MESH,
        )
    partner = chip * 2 + 1 - core
    pl.semaphore_signal(barrier, inc=1, device_id={"outer": partner}, device_id_type=MESH)

    for n in (0, 1):
        loads[n].wait()
    slot = slot_in[0, 0]
    rows = lax.broadcasted_iota(jnp.int32, embed.shape, 0)
    vector = jnp.sum(
        jnp.where(rows == slot, embed[...].astype(F32), 0.0), axis=0, keepdims=True
    )
    keyed[me] = (group[...].astype(F32) + vector).astype(BF16)
    pl.semaphore_wait(barrier, inner - 1 + chips)

    chain_k = Spread(keyed, k_up, k_down, k_recv, me, inner)
    chain_g = Spread(glob, g_up, g_down, g_recv, me, inner)
    chain_n = Spread(normed, n_up, n_down, n_recv, me, inner)
    sum_a = Scatter(term_a, relay_a, land_a, a_send, a_recv, a_pass, me, inner)
    sum_b = Scatter(term_b, relay_b, land_b, b_send, b_recv, b_pass, me, inner)

    chain_k.begin()

    for n in (2, 3, 4):
        loads[n].wait()
    merge_rows[...] = merge[...].astype(F32).reshape(merge_rows.shape)

    def put_query(cols, value):
        query[:, cols] = value.astype(BF16)

    multiply(lambda: merge[...], qw, put_query)

    for n in (5, 6):
        loads[n].wait()

    def keys_values(block):
        def put_key(cols, value):
            key_two[block, :, cols] = value.astype(BF16)

        def put_value(cols, value):
            value_two[block, :, cols] = value.astype(BF16)

        multiply(lambda: keyed[block], kw, put_key)
        multiply(lambda: keyed[block], vw, put_value)

    chain_g.begin()
    keys_values(me)
    for s in range(1, inner):
        if s == inner - 1:
            chain_k.step(s)

            @pl.when(me - s >= 0)
            def _():
                keys_values(me - s)

            @pl.when(me + s < inner)
            def _():
                keys_values(me + s)
        else:
            chain_k.step(s, keys_values)

    steps = list(range(1, inner))
    for h in range(heads):
        cols = slice(h * HEAD, (h + 1) * HEAD)
        mixed[:, cols] = attend_head(
            query[:, cols], flat(key_two[:, :, cols]), flat(value_two[:, :, cols])
        )
        if steps:
            chain_g.step(steps.pop(0))

    loads[7].wait()

    def put_term(term):
        def put(cols, value):
            term[:, :, cols] = value.reshape(
                inner, term.shape[1], value.shape[1]
            ).astype(BF16)

        return put

    multiply(lambda: mixed[...], ow, put_term(term_a))
    sum_a.run()

    for s in steps:
        chain_g.step(s)
    for n in (8, 9):
        loads[n].wait()

    def put_pair(start):
        def put(cols, value):
            shifted = pl.ds(pl.multiple_of(cols.start + start, HEAD), cols.size)
            pairs[place, :, shifted] = value.astype(BF16)

        return put

    multiply(lambda: flat(glob[...]), dk, put_pair(0))
    multiply(lambda: flat(glob[...]), dv, put_pair(width))

    def direct(hop):
        target = lax.rem(chip + hop, chips) * 2 + core
        return pltpu.make_async_remote_copy(
            src_ref=pairs.at[place], dst_ref=pairs.at[place],
            send_sem=p_send.at[hop], recv_sem=p_recv.at[place],
            device_id={"outer": target}, device_id_type=MESH,
        )

    def arrival(block):
        return pltpu.make_async_remote_copy(
            src_ref=pairs.at[block], dst_ref=pairs.at[block],
            send_sem=p_pass.at[0], recv_sem=p_recv.at[block],
            device_id={"outer": partner}, device_id_type=MESH,
        )

    def onward(hop):
        block = lax.rem(chip + hop, chips) * 2 + core
        return pltpu.make_async_remote_copy(
            src_ref=pairs.at[block], dst_ref=pairs.at[block],
            send_sem=p_pass.at[hop], recv_sem=p_recv.at[block],
            device_id={"outer": partner}, device_id_type=MESH,
        )

    for hop in range(1, chips):
        direct(hop).start()
    onward(0).start()

    sum_a.total(merge_rows[me], level)
    own = level[...]
    scale = lax.rsqrt(jnp.mean(own * own, axis=-1, keepdims=True) + 1e-6)
    normed[me] = (own * scale).astype(BF16)
    chain_n.begin()
    for hop in range(1, chips):
        arrival(lax.rem(chip + hop, chips) * 2 + core).wait_recv()
        onward(hop).start()
    for s in range(1, inner):
        chain_n.step(s)
    loads[10].wait()
    multiply(lambda: flat(normed[...]), dq, put_query)

    for hop in range(chips):
        arrival(lax.rem(chip + hop, chips) * 2 + 1 - core).wait_recv()

    for h in range(heads):
        cols = slice(h * HEAD, (h + 1) * HEAD)
        after = slice(width + h * HEAD, width + (h + 1) * HEAD)
        mixed[:, cols] = attend_head(
            query[:, cols], flat(pairs[:, :, cols]), flat(pairs[:, :, after])
        )
    loads[11].wait()
    multiply(lambda: mixed[...], do, put_term(term_b))
    sum_b.run()

    chain_k.drain()
    chain_g.drain()
    chain_n.drain()
    sum_a.drain()
    for hop in range(1, chips):
        direct(hop).wait_send()
    for hop in range(chips):
        onward(hop).wait_send()
    sum_b.total(level[...], level)
    out_ref[...] = level[...].astype(BF16)
    sum_b.drain()


def local(inner, outer, group, slot_ids, embed, merge, qw, kw, vw, ow, glob, dq, dk, dv, do):
    rows, depth = group.shape
    queries, wide = merge.shape
    width = qw.shape[1]
    own = queries // inner
    blocks = glob.shape[0] * inner
    dma = pltpu.SemaphoreType.DMA
    vmem = lambda *shape, kind=BF16: pltpu.VMEM(shape, kind)
    same = lambda array: pltpu.VMEM(array.shape, array.dtype)
    scratch = [
        same(embed), same(merge), same(group), same(qw), same(kw), same(vw), same(ow),
        same(dq), same(dk), same(dv), same(do),
        vmem(inner, rows, depth),
        vmem(inner, glob.shape[0], wide),
        vmem(inner, rows, width),
        vmem(inner, rows, width),
        vmem(queries, width),
        vmem(queries, width),
        vmem(inner, own, wide, kind=F32),
        vmem(own, wide, kind=F32),
        vmem(outer, blocks, 2 * width),
        vmem(inner, own, wide),
    ] + [vmem(inner, own, wide)] * 6 + [
        dma((12,)),
    ] + [dma((inner, 2)), dma((inner, 2)), dma((inner,))] * 3 + [dma((inner,))] * 6 + [dma((outer // 2,))] * 2 + [dma((outer,))]
    any_space = pl.BlockSpec(memory_space=pl.ANY)
    return pl.pallas_call(
        functools.partial(kernel, inner, outer),
        out_shape=jax.ShapeDtypeStruct((own, wide), BF16),
        in_specs=[pl.BlockSpec(memory_space=pltpu.SMEM)] + [any_space] * 12,
        out_specs=pl.BlockSpec(memory_space=pltpu.VMEM),
        scratch_shapes=scratch,
        compiler_params=pltpu.CompilerParams(
            collective_id=0, has_side_effects=True, vmem_limit_bytes=56 * 2 ** 20
        ),
    )(slot_ids, group, embed, merge, qw, kw, vw, ow, glob, dq, dk, dv, do)


def solution(mesh):
    rows = P(("outer", "inner"), None)
    split = P(None, "inner")
    down = P("inner", None)
    return jax.shard_map(
        functools.partial(local, mesh.shape["inner"], mesh.shape["outer"]),
        mesh=mesh,
        in_specs=(
            rows, P("outer", "inner"), P(), P(), split, split, split, down,
            rows, split, split, split, down,
        ),
        out_specs=rows,
        check_vma=False,
    )
```
